256 devices in a mesh: section: 4 (over y), fsdp: 16 (over x, z_hi, core), tp: 4 (over z_lo).
Axes of the slice: x: 4, y: 4, z: 8 (z_hi: 2, z_lo: 4; z = z_hi * 4 + z_lo), core: 2. Of those that a mesh axis runs over, the one named last changes fastest.
Arguments:
- image: bfloat16 [4, 12288, 4096], P('section', 'fsdp'), may hold values from -8 to 8
- text_states: bfloat16 [4, 1152, 4096], P('section', 'fsdp', 'tp'), may hold values from -6 to 6
- caption_lengths: int32 [16, 3], P('fsdp'), may hold values from 1 to 48, 72 in all within a row
- layer_map: int32 [4], replicated, may hold values from 0 to 3, each once
- w_qkv: bfloat16 [4, 4096, 3, 2048], P('section', 'fsdp', None, 'tp'), may hold values from -0.3125 to 0.3125
- w_text_kv: bfloat16 [4, 4096, 2, 2048], P('section', 'fsdp', None, 'tp'), may hold values from -0.09375 to 0.09375
- w_out: bfloat16 [4, 2048, 4096], P('section', 'tp', 'fsdp'), may hold values from -1.1953125 to 1.1953125
Outputs:
- attended: bfloat16 [4, 12288, 4096], P('section', 'fsdp', 'tp')
The draws below stay inside these ranges and needn't reach their ends.
Inputs may be any that keep to these rules, and one draw needn't show every extreme that they name: `caption_lengths`: each row sums to 72; every caption has at least one row. `layer_map`: a permutation of the sections.
All inputs are finite; a program needn't handle non-finite values.
Results may differ from the reference program's by a relative error of at most 0.02.
The reference program's roundings to bfloat16 on the way count: a program that leaves them out, or rounds other values in their place, can miss the bound.
Values may be sent and summed in bfloat16 or wider, within the bound.
No kernel may reach another device: no remote copies, remote signals or barrier semaphores. Data moves between devices by JAX's collectives and lax.ppermute only.
A program may use at most 128 MiB of HBM per device.

```python
import math
import jax
import jax.numpy as jnp
import numpy as np
from jax import lax

D = 4096
DT = 4096
HEADS = 16
HD = 128
IMG = 256
SAMP_DEV = 3
MAXCAP = 48
TXT_DEV = 72
ROWS = 12288
TXT = 1152
N_SECTION = 4
N_FSDP = 16
N_TP = 4


def draw_image(key, part):
    key = jax.random.fold_in(key, 11)
    lead_key = jax.random.fold_in(key, 0)
    values = jax.random.normal(lead_key, (N_SECTION, ROWS, D), jnp.float32)
    return jnp.clip(values, -8.0, 8.0).astype(jnp.bfloat16)


def draw_w_qkv(key, part):
    key = jax.random.fold_in(key, 23)
    base_key = jax.random.fold_in(key, 0)
    values = jax.random.normal(base_key, (N_SECTION, D, 3, HEADS * HD), jnp.float32) * D ** (-0.5)
    bound = 20.0 * D ** (-0.5)
    return jnp.clip(values, -bound, bound).astype(jnp.bfloat16)


def steps_of(rng, dims, shards, smallest, top_value):
    level = 1.0
    for axis_at, parts in shards:
        steps = jax.random.uniform(jax.random.fold_in(jax.random.fold_in(rng, 6), axis_at), (parts,), jnp.float32, smallest / len(shards), top_value / len(shards))
        level = level * jnp.repeat(jnp.exp(steps), dims[axis_at] // parts).reshape((-1,) + (1,) * (len(dims) - 1 - axis_at))
    return level


def split_up(amount, total, most, skew):
    loads = [(1 << 20) // math.isqrt(grade ** skew) + 1 for grade in range(2, amount + 1)]
    surplus, counts = total - most - (amount - 1), [1] * (amount - 1)
    while surplus > 0:
        candidates = [i for i in range(amount - 1) if counts[i] < most]
        whole, budget = sum([loads[i] for i in candidates]), surplus
        for i in candidates:
            extra = min(most - counts[i], max(1, budget * loads[i] // whole), surplus)
            counts[i] = counts[i] + extra
            surplus = surplus - extra
    return np.array([most] + counts)


def ragged(own_key, number_of, total, most, lean):
    if number_of == 2:
        one = jax.random.randint(own_key, (), max(1, total - most), min(most, total - 1) + 1)
        return jnp.stack([one, total - one])
    sizes = jnp.asarray(split_up(number_of, total, most, lean), jnp.int32)
    couples = (number_of - 1) // 2
    giver, receiver = sizes[1:1 + 2 * couples:2], sizes[2:2 + 2 * couples:2]
    room = jnp.minimum(giver - 1, most - receiver)
    shifted = jax.random.randint(jax.random.fold_in(own_key, 1), (couples,), 0, 1 << 20) % (room + 1)
    sizes = sizes.at[1:1 + 2 * couples:2].set(giver - shifted).at[2:2 + 2 * couples:2].set(receiver + shifted)
    return sizes[jax.random.permutation(jax.random.fold_in(own_key, 2), number_of)]


def centred(own_key, dims, width, most, cuts=(), kind=jnp.bfloat16):
    level = steps_of(own_key, dims, cuts, -0.22, 0.18) if cuts else 1.0
    array = jax.random.normal(own_key, dims, jnp.float32) * width * level
    return jnp.minimum(jnp.maximum(array, -most), most).astype(kind)


def setup_inputs(seed: int = 0) -> dict:
    keys = jax.random.split(jax.random.key(seed), 8)
    image = draw_image(jax.random.fold_in(keys[7], 71), 0)
    text_states = centred(keys[1], (N_SECTION, TXT, DT), 1.0, 6.0, ((0, 4), (1, 16), (2, 4)))
    caption_lengths = jax.vmap(lambda own: ragged(own, SAMP_DEV, TXT_DEV, MAXCAP, 2))(jax.random.split(keys[2], N_FSDP)).reshape((N_FSDP, SAMP_DEV)).astype(jnp.int32)
    layer_map = jax.random.permutation(keys[3], N_SECTION).astype(jnp.int32)
    w_qkv = draw_w_qkv(jax.random.fold_in(keys[7], 71), 0)
    w_text_kv = centred(keys[5], (N_SECTION, DT, 2, HEADS * HD), DT ** -0.5, 0.09375, ((0, 4), (1, 16), (3, 4)))
    w_out = centred(keys[6], (N_SECTION, HEADS * HD, D), 0.2, 1.1953125, ((0, 4), (1, 4), (2, 16)))
    return dict(image=image, text_states=text_states, caption_lengths=caption_lengths, layer_map=layer_map, w_qkv=w_qkv, w_text_kv=w_text_kv, w_out=w_out)


def caption_visible(image_count, text_count, lengths):
    sample_image = jnp.arange(image_count, dtype=jnp.int32) // IMG
    boundary = jnp.cumsum(lengths).astype(jnp.int32)[:-1]
    positions = jnp.arange(text_count, dtype=jnp.int32)
    caption_of = jnp.sum((positions[:, None] >= boundary[None, :]).astype(jnp.int32), axis=1).astype(jnp.int32)
    image_seen = sample_image[:, None] == sample_image[None, :]
    text_seen = sample_image[:, None] == caption_of[None, :]
    return jnp.concatenate([image_seen, text_seen], axis=1)


def masked_attention(queries, key_image, value_image, key_text, value_text, lengths):
    keys_all = jnp.concatenate([key_image, key_text], axis=0)
    values_all = jnp.concatenate([value_image, value_text], axis=0)
    scores = jnp.einsum("qhd,khd->hqk", queries.astype(jnp.float32), keys_all.astype(jnp.float32)) * (HD ** -0.5)
    visible = caption_visible(queries.shape[0], key_text.shape[0], lengths)[None]
    highest = jnp.max(jnp.where(visible, scores, -jnp.inf), axis=-1, keepdims=True)
    raised = jnp.where(visible, jnp.exp(scores - highest), jnp.float32(0.0))
    weights = (raised / jnp.sum(raised, axis=-1, keepdims=True)).astype(jnp.bfloat16)
    mixed = jnp.einsum("hqk,khd->qhd", weights.astype(jnp.float32), values_all.astype(jnp.float32))
    return mixed.astype(jnp.bfloat16).reshape(queries.shape[0], -1)


def reference(image, text_states, caption_lengths, layer_map, w_qkv, w_text_kv, w_out):
    head_width = (HEADS // N_TP) * HD
    image_group = SAMP_DEV * IMG
    results = []
    for section_id in range(N_SECTION):
        text = jnp.take(text_states, layer_map[section_id], axis=0)
        qkv = jnp.dot(image[section_id], w_qkv[section_id].reshape(D, 3 * HEADS * HD), preferred_element_type=jnp.float32)
        qkv = qkv.astype(jnp.bfloat16).reshape(-1, 3, HEADS, HD)
        text_kv = jnp.dot(text, w_text_kv[section_id].reshape(DT, 2 * HEADS * HD), preferred_element_type=jnp.float32)
        text_kv = text_kv.astype(jnp.bfloat16).reshape(-1, 2, HEADS, HD)

        def one_group(group_id):
            image_part = lax.dynamic_slice_in_dim(qkv, group_id * image_group, image_group, 0)
            text_part = lax.dynamic_slice_in_dim(text_kv, group_id * TXT_DEV, TXT_DEV, 0)
            lengths = lax.dynamic_index_in_dim(caption_lengths, group_id, 0, keepdims=False)
            return masked_attention(image_part[:, 0], image_part[:, 1], image_part[:, 2], text_part[:, 0], text_part[:, 1], lengths)

        mixed = lax.map(one_group, jnp.arange(N_FSDP, dtype=jnp.int32)).reshape(-1, HEADS * HD)
        summed = jnp.zeros((mixed.shape[0], D), jnp.float32)
        for block_id in range(N_TP):
            term = jnp.dot(mixed[:, block_id * head_width:(block_id + 1) * head_width],
                           w_out[section_id, block_id * head_width:(block_id + 1) * head_width, :],
                           preferred_element_type=jnp.float32)
            rounded = lax.optimization_barrier(term.astype(jnp.bfloat16))
            summed = summed + rounded.astype(jnp.float32)
        results.append(summed.astype(jnp.bfloat16))
    return jnp.stack(results)
```

```python
import functools

import jax
import jax.numpy as jnp
from jax import lax
from jax.experimental import pallas as pl
from jax.experimental.pallas import tpu as pltpu
from jax.sharding import PartitionSpec as P

HD = 128
IMG = 256
NX, NZ, LINE = 4, 8, 4
TROWS = 80
BF16 = jnp.bfloat16
F32 = jnp.float32
AXES = ("fsdp", "tp")


def place(x, z, core):
    return ((x * 2 + z // LINE) * 2 + core) * LINE + z % LINE


def shift(value, dx=0, dz=0, dcore=0, chosen=None):
    pairs = []
    for x in range(NX):
        for z in range(NZ):
            if chosen is not None and not chosen(x, z):
                continue
            for core in range(2):
                to = place((x + dx) % NX, (z + dz) % NZ, (core + dcore) % 2)
                pairs.append((place(x, z, core), to))
    return lax.ppermute(value, AXES, pairs)


def rotate(value, axis, step):
    return lax.ppermute(value, axis, [(i, (i + step) % 4) for i in range(4)])


def x_ring(block):
    half = block.shape[0] // 2
    from_left = shift(block, dx=1)
    from_right = shift(block, dx=-1)
    far_top = shift(from_left[:half], dx=1)
    far_bottom = shift(from_right[half:], dx=-1)
    return [block, from_left, from_right, far_top, far_bottom]


def block_parts(refs):
    out = []
    for group in range(2):
        own, left, right, top, bottom = refs[5 * group:5 * group + 5]
        half = own.shape[0] // 2
        for ref in (own, left, right):
            out += [ref.at[pl.ds(0, half)], ref.at[pl.ds(half, half)]]
        out += [top, bottom]
    return out


def head_kernel(table, columns, lengths, image_own, image_other, text_own, text_other, *rest):
    weights, (out, w, rows, text, tkv, w_sem, t_sem, i_sem) = rest[:10], rest[10:]
    depth = 256
    copies = []
    for j, part in enumerate(block_parts(weights)):
        at = pl.multiple_of(table[j] * depth, depth)
        copies.append(pltpu.make_async_copy(part, w.at[pl.ds(at, depth)], w_sem.at[j]))
    for g, source in enumerate((text_own, text_other)):
        for r in range(LINE):
            at = pl.multiple_of(columns[r] * 1024, 1024)
            copies.append(pltpu.make_async_copy(
                source.at[r], text.at[pl.ds(g * TROWS, TROWS), pl.ds(at, 1024)],
                t_sem.at[g * LINE + r]))
    for copy in copies:
        copy.start()
    for k in range(6):
        source = image_own if k < 3 else image_other
        pltpu.make_async_copy(
            source.at[pl.ds((k % 3) * IMG, IMG)], rows.at[k], i_sem.at[k]).start()
    for copy in copies:
        copy.wait()
    text_kv = jnp.dot(text[...], w[:, 3 * HD:], preferred_element_type=F32).astype(BF16)
    tkv[...] = jnp.zeros_like(tkv)
    for g in range(2):
        tkv[g, 0:TROWS, :] = text_kv[g * TROWS:(g + 1) * TROWS]

    def sample(k, carry):
        pltpu.make_async_copy(image_own.at[pl.ds(0, IMG)], rows.at[k], i_sem.at[k]).wait()
        qkv = jnp.dot(rows[k], w[:, :3 * HD], preferred_element_type=F32).astype(BF16)
        q, key, value = qkv[:, :HD], qkv[:, HD:2 * HD], qkv[:, 2 * HD:]
        g = k // 3
        j = k - 3 * g
        first = lengths[g, 0]
        second = first + lengths[g, 1]
        low = jnp.where(j == 0, 0, jnp.where(j == 1, first, second))
        high = jnp.where(j == 0, first, jnp.where(j == 1, second, 72))
        tk, tv = tkv[g, :, :HD], tkv[g, :, HD:]
        dims = (((1,), (1,)), ((), ()))
        scale = HD ** (-0.5)
        s_image = lax.dot_general(q, key, dims, preferred_element_type=F32) * scale
        s_text = lax.dot_general(q, tk, dims, preferred_element_type=F32) * scale
        position = lax.broadcasted_iota(jnp.int32, s_text.shape, 1)
        seen = (position >= low) & (position < high)
        s_text = jnp.where(seen, s_text, -jnp.inf)
        top = jnp.maximum(jnp.max(s_image, axis=1, keepdims=True),
                          jnp.max(s_text, axis=1, keepdims=True))
        e_image = jnp.exp(s_image - top)
        e_text = jnp.exp(s_text - top)
        total = (jnp.sum(e_image, axis=1, keepdims=True)
                 + jnp.sum(e_text, axis=1, keepdims=True))
        inverse = 1.0 / total
        mixed = jnp.dot((e_image * inverse).astype(BF16), value, preferred_element_type=F32)
        mixed += jnp.dot((e_text * inverse).astype(BF16), tv, preferred_element_type=F32)
        out[k] = mixed.astype(BF16)
        return carry

    lax.fori_loop(0, 6, sample, 0)


def attend(table, columns, lengths, images, texts, weights):
    smem = pl.BlockSpec(memory_space=pltpu.SMEM)
    hbm = pl.BlockSpec(memory_space=pl.ANY)
    return pl.pallas_call(
        head_kernel,
        out_shape=jax.ShapeDtypeStruct((6, IMG, HD), BF16),
        in_specs=[smem] * 3 + [hbm] * 14,
        out_specs=pl.BlockSpec(memory_space=pltpu.VMEM),
        scratch_shapes=[
            pltpu.VMEM((4096, 5 * HD), BF16),
            pltpu.VMEM((6, IMG, 4096), BF16),
            pltpu.VMEM((2 * TROWS, 4096), BF16),
            pltpu.VMEM((2, 128, 2 * HD), BF16),
            pltpu.SemaphoreType.DMA((16,)),
            pltpu.SemaphoreType.DMA((8,)),
            pltpu.SemaphoreType.DMA((6,)),
        ],
        compiler_params=pltpu.CompilerParams(vmem_limit_bytes=48 * 2**20),
        cost_estimate=pl.CostEstimate(
            flops=2 * 1536 * 4096 * 640, bytes_accessed=18 * 2**20, transcendentals=6 * 256 * 384),
    )(table, columns, lengths, *images, *texts, *weights)


def out_kernel(spots, heads, *rest):
    mixed_parts, rest = rest[:8], rest[8:]
    stacks, (out, w, m, w_sem, m_sem) = rest[:4], rest[4:]
    copies = []
    for i, stack in enumerate(stacks):
        for d in range(4):
            n = 4 * i + d
            at = pl.multiple_of(spots[n, 1] * 256, 256)
            copies.append(pltpu.make_async_copy(
                stack.at[d], w.at[spots[n, 0], :, pl.ds(at, 256)], w_sem.at[n]))
    for h in range(2):
        for r in range(LINE):
            for s in range(2):
                at = pl.multiple_of((heads[4 + s] + h) * HD, HD)
                copies.append(pltpu.make_async_copy(
                    mixed_parts[4 * h + r].at[:, pl.ds(s * HD, HD)],
                    m.at[heads[r], :, pl.ds(at, HD)], m_sem.at[(4 * h + r) * 2 + s]))
    for copy in copies:
        copy.start()
    for copy in copies:
        copy.wait()

    def tile(k, carry):
        at = pl.ds(pl.multiple_of(k * 256, 256), 256)
        total = jnp.zeros((256, 1024), F32)
        for block in range(LINE):
            term = jnp.dot(m[block, at, :], w[block], preferred_element_type=F32)
            total += term.astype(BF16).astype(F32)
        out[at, :] = total.astype(BF16)
        return carry

    lax.fori_loop(0, 3, tile, 0)


def project(spots, heads, mixed_parts, stacks):
    smem = pl.BlockSpec(memory_space=pltpu.SMEM)
    hbm = pl.BlockSpec(memory_space=pl.ANY)
    return pl.pallas_call(
        out_kernel,
        out_shape=jax.ShapeDtypeStruct((768, 1024), BF16),
        in_specs=[smem] * 2 + [hbm] * 12,
        out_specs=pl.BlockSpec(memory_space=pltpu.VMEM),
        scratch_shapes=[
            pltpu.VMEM((LINE, 512, 1024), BF16),
            pltpu.VMEM((LINE, 768, 512), BF16),
            pltpu.SemaphoreType.DMA((16,)),
            pltpu.SemaphoreType.DMA((16,)),
        ],
        compiler_params=pltpu.CompilerParams(vmem_limit_bytes=48 * 2**20),
        cost_estimate=pl.CostEstimate(
            flops=2 * 768 * 2048 * 1024, bytes_accessed=9 * 2**20, transcendentals=0),
    )(spots, heads, *mixed_parts, *stacks)


def body(image, text_states, caption_lengths, layer_map, w_qkv, w_text_kv, w_out):
    y = lax.axis_index("section")
    f = lax.axis_index("fsdp")
    t = lax.axis_index("tp")
    x, z, core = f // 4, (f // 2) % 2 * LINE + t, f % 2

    both = jnp.concatenate(
        [w_qkv[0].reshape(256, 3, 4, HD), w_text_kv[0].reshape(256, 2, 4, HD)], axis=1)

    def head_block(head):
        return lax.dynamic_index_in_dim(both, head, 2, keepdims=False).reshape(256, 5 * HD)

    gathered = []
    for h in range(2):
        swapped = shift(head_block(2 * (1 - core) + h), dcore=1)
        own = jnp.concatenate([head_block(2 * core + h), swapped], axis=0)
        gathered.append(x_ring(own) + x_ring(shift(own, dz=4)))

    chosen = lax.dynamic_index_in_dim(layer_map, y, 0, keepdims=False)
    text_here = jnp.pad(text_states[0], ((0, TROWS - 72), (0, 0)))
    options = [text_here] + [rotate(text_here, "section", -r) for r in (1, 2, 3)]
    picked = lax.select_n((chosen - y) % 4, *options)
    text_own = jnp.stack([picked] + [rotate(picked, "tp", r) for r in (1, 2, 3)])
    texts = [text_own, shift(text_own, dcore=1)]
    columns = jnp.stack([(t - r) % 4 for r in range(4)]).astype(jnp.int32)

    images = [image[0], shift(image[0], dcore=1)]
    lengths = jnp.concatenate([caption_lengths, shift(caption_lengths, dcore=1)], axis=0)

    table = []
    for group in range(2):
        for dx in (0, -1, 1, 2):
            chip = ((x + dx) % 4) * 4 + (z // LINE + group) % 2 * 2
            table += [chip + core, chip + 1 - core]
    table = jnp.stack(table).astype(jnp.int32)

    blocks = [w_out[0]] + [
        shift(w_out[0], dz=d, chosen=lambda a, b, d=d: (b + d) % NZ % LINE == a)
        for d in range(1, NZ)]
    first, last = jnp.stack(blocks[:4]), jnp.stack(blocks[4:])
    away = (x - t) % 4
    right1 = shift(first, dx=1, chosen=lambda a, b: a == b % LINE)
    left1 = shift(last, dx=-1, chosen=lambda a, b: a == b % LINE)
    right2 = shift(lax.select(away == 0, last, right1), dx=1,
                   chosen=lambda a, b: (a - b) % 4 in (0, 1))
    left2 = shift(lax.select(away == 0, first, left1), dx=-1,
                  chosen=lambda a, b: (a - b) % 4 in (0, 3))
    first = lax.select_n(away, first, right1, right2, left2)
    last = lax.select_n(away, last, right2, left2, left1)
    stacks = [first, last, shift(first, dcore=1), shift(last, dcore=1)]
    spots = []
    for other in range(2):
        for d in range(NZ):
            source = (z - d) % NZ
            spots.append(jnp.stack([source % LINE, source // LINE * 2 + (core + other) % 2]))
    spots = jnp.stack(spots).astype(jnp.int32)

    mixed_parts = []
    for h in range(2):
        mixed = attend(table, columns, lengths, images, texts, gathered[h])
        swapped = shift(mixed[3:].reshape(768, HD), dcore=1)
        mine = jnp.concatenate([mixed[:3].reshape(768, HD), swapped], axis=1)
        mixed_parts += [mine] + [rotate(mine, "tp", r) for r in (1, 2, 3)]
    heads = jnp.concatenate(
        [columns, jnp.stack([2 * core, 2 - 2 * core]).astype(jnp.int32)])
    return project(spots, heads, mixed_parts, stacks)[None]


def solution(mesh):
    return jax.shard_map(
        body,
        mesh=mesh,
        in_specs=(
            P("section", "fsdp", None),
            P("section", "fsdp", "tp"),
            P("fsdp", None),
            P(),
            P("section", "fsdp", None, "tp"),
            P("section", "fsdp", None, "tp"),
            P("section", "tp", "fsdp"),
        ),
        out_specs=P("section", "fsdp", "tp"),
        check_vma=False,
    )
```

```python
import functools

import jax
import jax.numpy as jnp
from jax import lax
from jax.experimental import pallas as pl
from jax.experimental.pallas import tpu as pltpu
from jax.sharding import PartitionSpec as P

HD = 128
IMG = 256
NX, NZ, LINE = 4, 8, 4
LOG2E = 1.4426950408889634
TROWS = 80
BF16 = jnp.bfloat16
F32 = jnp.float32
AXES = ("fsdp", "tp")


def place(x, z, core):
    return ((x * 2 + z // LINE) * 2 + core) * LINE + z % LINE


def shift(value, dx=0, dz=0, dcore=0):
    pairs = []
    for x in range(NX):
        for z in range(NZ):
            for core in range(2):
                to = place((x + dx) % NX, (z + dz) % NZ, (core + dcore) % 2)
                pairs.append((place(x, z, core), to))
    return lax.ppermute(value, AXES, pairs)


def rotate(value, axis, step):
    return lax.ppermute(value, axis, [(i, (i + step) % 4) for i in range(4)])


def after(value, *others):
    return lax.optimization_barrier((value, *others))[0] if others else value


def transposed(value, dz=0):
    pairs = []
    for x in range(NX):
        for z in range(NZ):
            for core in range(2):
                to = place(z % LINE, (z // LINE * LINE + x + dz) % NZ, core)
                pairs.append((place(x, z, core), to))
    return lax.ppermute(value, AXES, pairs)


def x_all(block, *gate):
    block = after(block, *gate)
    return [block] + [shift(block, dx=d) for d in (1, -1, 2)]


def x_gather(block):
    return lax.all_gather(
        block, "fsdp", axis_index_groups=[[4 * x + rest for x in range(NX)] for rest in range(4)])


def block_parts(refs, depth):
    out = []
    for ref in refs:
        for view in [ref] if len(ref.shape) == 2 else [ref.at[i] for i in range(ref.shape[0])]:
            out += [view.at[pl.ds(i * depth, depth)] for i in range(view.shape[0] // depth)]
    return out


def text_kernel(table, text_own, text_other, from_low, from_high, *rest):
    outs, (w, text, w_sem, t_sem) = rest[:4], rest[4:]
    copies = []
    for j, part in enumerate(block_parts((from_low, from_high), 256)):
        at = pl.multiple_of(table[j] * 256, 256)
        copies.append(pltpu.make_async_copy(part, w.at[pl.ds(at, 256)], w_sem.at[j]))
    for g, source in enumerate((text_own, text_other)):
        for r in range(4):
            copies.append(pltpu.make_async_copy(
                source.at[-r % 4], text.at[r, pl.ds(g * TROWS, TROWS)], t_sem.at[4 * g + r]))
    for copy in copies:
        copy.start()
    for copy in copies:
        copy.wait()
    for r in range(4):
        outs[r][...] = jnp.dot(
            text[r], w[...], preferred_element_type=F32).astype(outs[r].dtype)


def project_text(table, texts, weights):
    smem = pl.BlockSpec(memory_space=pltpu.SMEM)
    hbm = pl.BlockSpec(memory_space=pl.ANY)
    return pl.pallas_call(
        text_kernel,
        out_shape=[jax.ShapeDtypeStruct((2 * TROWS, 4 * HD), F32 if r == 0 else BF16)
                   for r in range(4)],
        in_specs=[smem] + [hbm] * 4,
        out_specs=[pl.BlockSpec(memory_space=pltpu.VMEM)] * 4,
        scratch_shapes=[
            pltpu.VMEM((1024, 4 * HD), BF16),
            pltpu.VMEM((4, 2 * TROWS, 1024), BF16),
            pltpu.SemaphoreType.DMA((4,)),
            pltpu.SemaphoreType.DMA((8,)),
        ],
        compiler_params=pltpu.CompilerParams(vmem_limit_bytes=24 * 2**20),
        cost_estimate=pl.CostEstimate(
            flops=2 * 640 * 1024 * 512, bytes_accessed=4 * 2**20, transcendentals=0),
    )(table, *texts, *weights)


def head_kernel(side, table, lengths, image_own, image_other, *rest):
    parts, weights = rest[:4], rest[4:-10]
    out, w, rows, text, sent, tkv, qkv, w_sem, t_sem, i_sem = rest[-10:]
    depth = 256
    copies = []
    for j, part in enumerate(block_parts(weights, depth)):
        at = pl.multiple_of(table[j] * depth, depth)
        copies.append(pltpu.make_async_copy(part, w.at[pl.ds(at, depth)], w_sem.at[j]))
    for r in range(4):
        copies.append(pltpu.make_async_copy(
            parts[r].at[:, pl.ds(side * 2 * HD, 2 * HD)], text if r == 0 else sent.at[r - 1],
            t_sem.at[r]))
    for copy in copies:
        copy.start()
    for k in range(6):
        source = image_own if k < 3 else image_other
        pltpu.make_async_copy(
            source.at[pl.ds((k % 3) * IMG, IMG)],
            rows.at[k // 3, pl.ds((k % 3) * IMG, IMG)], i_sem.at[k]).start()
    for copy in copies:
        copy.wait()
    text_kv = (text[...] + sent[0].astype(F32) + sent[1].astype(F32)
               + sent[2].astype(F32)).astype(BF16)
    tkv[...] = jnp.zeros_like(tkv)
    for g in range(2):
        tkv[g, 0:TROWS, :] = text_kv[g * TROWS:(g + 1) * TROWS]

    def load(k):
        g = k // 3
        here = pl.ds(pl.multiple_of((k - 3 * g) * IMG, IMG), IMG)
        pltpu.make_async_copy(
            image_own.at[pl.ds(0, IMG)], rows.at[g, here], i_sem.at[k]).wait()

    def compute(k):
        g = k // 3
        here = pl.ds(pl.multiple_of((k - 3 * g) * IMG, IMG), IMG)
        qkv[k % 2] = jnp.dot(rows[g, here], w[...], preferred_element_type=F32).astype(BF16)

    def mix(k):
        g = k // 3
        j = k - 3 * g
        q, key, value = qkv[k % 2, :, :HD], qkv[k % 2, :, HD:2 * HD], qkv[k % 2, :, 2 * HD:]
        first = lengths[g, 0]
        second = first + lengths[g, 1]
        low = jnp.where(j == 0, 0, jnp.where(j == 1, first, second))
        high = jnp.where(j == 0, first, jnp.where(j == 1, second, 72))
        tk, tv = tkv[g, :, :HD], tkv[g, :, HD:]
        dims = (((1,), (1,)), ((), ()))
        scale = HD ** (-0.5) * LOG2E
        s_image = lax.dot_general(q, key, dims, preferred_element_type=F32) * scale
        s_text = lax.dot_general(q, tk, dims, preferred_element_type=F32) * scale
        position = lax.broadcasted_iota(jnp.int32, s_text.shape, 1)
        seen = (position >= low) & (position < high)
        s_text = jnp.where(seen, s_text, -jnp.inf)
        top = jnp.maximum(jnp.max(s_image, axis=1, keepdims=True),
                          jnp.max(s_text, axis=1, keepdims=True))
        e_image = jnp.exp2(s_image - top)
        e_text = jnp.exp2(s_text - top)
        total = (jnp.sum(e_image, axis=1, keepdims=True)
                 + jnp.sum(e_text, axis=1, keepdims=True))
        inverse = 1.0 / total
        mixed = jnp.dot((e_image * inverse).astype(BF16), value, preferred_element_type=F32)
        mixed += jnp.dot((e_text * inverse).astype(BF16), tv, preferred_element_type=F32)
        out[k] = mixed.astype(BF16)

    load(0)
    compute(0)

    def step(k, carry):
        load(k + 1)
        compute(k + 1)
        mix(k)
        return carry

    lax.fori_loop(0, 5, step, 0)
    mix(5)


def attend(side, table, lengths, images, parts, weights):
    smem = pl.BlockSpec(memory_space=pltpu.SMEM)
    hbm = pl.BlockSpec(memory_space=pl.ANY)
    return pl.pallas_call(
        functools.partial(head_kernel, side),
        out_shape=jax.ShapeDtypeStruct((6, IMG, HD), BF16),
        in_specs=[smem] * 2 + [hbm] * (6 + len(weights)),
        out_specs=pl.BlockSpec(memory_space=pltpu.VMEM),
        scratch_shapes=[
            pltpu.VMEM((4096, 3 * HD), BF16),
            pltpu.VMEM((2, 3 * IMG, 4096), BF16),
            pltpu.VMEM((2 * TROWS, 2 * HD), F32),
            pltpu.VMEM((3, 2 * TROWS, 2 * HD), BF16),
            pltpu.VMEM((2, 128, 2 * HD), BF16),
            pltpu.VMEM((2, IMG, 3 * HD), BF16),
            pltpu.SemaphoreType.DMA((16,)),
            pltpu.SemaphoreType.DMA((4,)),
            pltpu.SemaphoreType.DMA((6,)),
        ],
        compiler_params=pltpu.CompilerParams(vmem_limit_bytes=48 * 2**20),
        cost_estimate=pl.CostEstimate(
            flops=2 * 1536 * 4096 * 512, bytes_accessed=16 * 2**20, transcendentals=6 * 256 * 384),
    )(table, lengths, *images, *parts, *weights)


def out_kernel(spots, heads, *rest):
    mixed_parts, rest = rest[:2], rest[2:]
    stacks, (out, w, m, total, w_sem, m_sem) = rest[:2], rest[2:]
    w_copies, m_copies = [], []
    for n, part in enumerate(block_parts(stacks, 512)):
        at = pl.multiple_of(spots[n, 1] * 256, 256)
        w_copies.append(pltpu.make_async_copy(
            part, w.at[spots[n, 0], :, pl.ds(at, 256)], w_sem.at[n]))
    for r in range(LINE):
        for h in range(2):
            for s in range(2):
                at = pl.multiple_of((heads[s] + h) * HD, HD)
                m_copies.append(pltpu.make_async_copy(
                    mixed_parts[h].at[r, :, pl.ds(s * HD, HD)],
                    m.at[r, :, pl.ds(at, HD)], m_sem.at[4 * r + 2 * h + s]))
    for copy in w_copies + m_copies:
        copy.start()
    for copy in w_copies:
        copy.wait()
    for r in range(LINE):
        for copy in m_copies[4 * r:4 * r + 4]:
            copy.wait()
        for k in range(3):
            at = slice(256 * k, 256 * k + 256)
            term = jnp.dot(m[r, at, :], w[(r + 2) % LINE], preferred_element_type=F32)
            term = term.astype(BF16).astype(F32)
            if r == 0:
                total[at, :] = term
            elif r < LINE - 1:
                total[at, :] += term
            else:
                out[at, :] = (total[at, :] + term).astype(BF16)


def project(spots, heads, mixed_parts, stacks):
    smem = pl.BlockSpec(memory_space=pltpu.SMEM)
    hbm = pl.BlockSpec(memory_space=pl.ANY)
    return pl.pallas_call(
        out_kernel,
        out_shape=jax.ShapeDtypeStruct((768, 1024), BF16),
        in_specs=[smem] * 2 + [hbm] * 4,
        out_specs=pl.BlockSpec(memory_space=pltpu.VMEM),
        scratch_shapes=[
            pltpu.VMEM((LINE, 512, 1024), BF16),
            pltpu.VMEM((LINE, 768, 512), BF16),
            pltpu.VMEM((768, 1024), F32),
            pltpu.SemaphoreType.DMA((16,)),
            pltpu.SemaphoreType.DMA((16,)),
        ],
        compiler_params=pltpu.CompilerParams(vmem_limit_bytes=48 * 2**20),
        cost_estimate=pl.CostEstimate(
            flops=2 * 768 * 2048 * 1024, bytes_accessed=9 * 2**20, transcendentals=0),
    )(spots, heads, *mixed_parts, *stacks)


def body(image, text_states, caption_lengths, layer_map, w_qkv, w_text_kv, w_out):
    y = lax.axis_index("section")
    f = lax.axis_index("fsdp")
    t = lax.axis_index("tp")
    x, z, core = f // 4, (f // 2) % 2 * LINE + t, f % 2

    image_weight = w_qkv[0].reshape(256, 3, 4, HD)
    text_weight = w_text_kv[0].reshape(256, 2, 4, HD)

    def head_columns(side):
        heads = [2 * side, 2 * side + 1]
        return jnp.concatenate(
            [image_weight[:, i, n] for n in heads for i in range(3)]
            + [text_weight[:, i, n] for n in heads for i in range(2)], axis=1)

    side0, side1 = head_columns(0), head_columns(1)
    sent = jnp.concatenate(
        [lax.select(core == 0, side1, side0),
         jnp.pad(caption_lengths.astype(BF16), ((0, 15), (0, 10 * HD - 3)))])
    got = shift(sent, dcore=1)
    lengths = jnp.concatenate([caption_lengths, got[256:257, :3].astype(jnp.int32)])
    both = jnp.concatenate([lax.select(core == 0, side0, side1), got[:256]])
    cuts = [both[:, :3 * HD], both[:, 3 * HD:6 * HD], both[:, 6 * HD:]]

    chosen = lax.dynamic_index_in_dim(layer_map, y, 0, keepdims=False)
    text_here = jnp.pad(text_states[0], ((0, TROWS - 72), (0, 0)))
    options = [text_here] + [rotate(text_here, "section", -r) for r in (1, 2, 3)]
    picked = lax.select_n((chosen - y) % 4, *options)

    def z_pair(block, *gate):
        block = after(block, *gate)
        return [shift(block, dz=2), shift(block, dz=-2)]

    wide = jnp.stack([picked] + [rotate(picked, "tp", r) for r in (1, 2, 3)])
    pair0 = z_pair(cuts[0], got, picked)

    weights0 = x_gather(jnp.concatenate(pair0))
    slices = [lax.dynamic_index_in_dim(wide, (t - x - d) % 4, 0, keepdims=False) for d in range(4)]
    text_own = jnp.stack(slices[:1] + [shift(slices[d], dx=d) for d in (1, 2, 3)])
    pair_text = z_pair(cuts[2], wide, *pair0)
    images = [image[0], shift(after(image[0], wide, got), dcore=1)]

    texts = [text_own, shift(after(text_own, *pair_text), dcore=1)]

    def rows_at(source, dz):
        chip = source % 4 * 4 + (z + dz) % NZ // LINE * 2
        return [chip + core, chip + 1 - core]

    def table_of(sources):
        rows = [row for source in sources for dz in (-2, 2) for row in rows_at(source, dz)]
        return jnp.stack(rows).astype(jnp.int32)

    text_parts = list(project_text(table_of([x]) % 4, texts, pair_text))
    text_parts = text_parts[:1] + [shift(text_parts[r], dx=r) for r in (1, 2, 3)]
    pair1 = z_pair(cuts[1], texts[1])

    weights1 = x_gather(jnp.concatenate(pair1))
    w_out_here = after(w_out[0], *text_parts[1:])
    pieces = jnp.concatenate([transposed(w_out_here), transposed(w_out_here, dz=4)])
    mixed0 = attend(
        0, table_of(range(NX)), lengths, images,
        [text_parts[0], *after(tuple(text_parts[1:]), *pair1)], [weights0])

    def swap_rows(mixed):
        swapped = shift(mixed[3:].reshape(768, HD), dcore=1)
        return jnp.concatenate([mixed[:3].reshape(768, HD), swapped], axis=1)

    mine0 = swap_rows(mixed0)
    mixed1 = attend(
        1, after(table_of(range(NX)), mine0, pieces), lengths, images, text_parts, [weights1])

    mine1 = swap_rows(mixed1)
    mixed_parts = [lax.all_gather(mine0, "tp"), lax.all_gather(mine1, "tp")]
    stack = jnp.concatenate(x_all(pieces, mine1))
    stacks = [stack, shift(stack, dcore=1)]
    spots = []
    for other in range(2):
        for dx in (0, -1, 1, 2):
            for dz in (0, 4):
                spots.append(jnp.stack(
                    [(x + dx) % 4, (z + dz) % NZ // LINE * 2 + (core + other) % 2]))
    spots = jnp.stack(spots).astype(jnp.int32)
    heads = jnp.stack([2 * core, 2 - 2 * core]).astype(jnp.int32)
    return project(spots, heads, mixed_parts, stacks)[None]


def solution(mesh):
    return jax.shard_map(
        body,
        mesh=mesh,
        in_specs=(
            P("section", "fsdp", None),
            P("section", "fsdp", "tp"),
            P("fsdp", None),
            P(),
            P("section", "fsdp", None, "tp"),
            P("section", "fsdp", None, "tp"),
            P("section", "tp", "fsdp"),
        ),
        out_specs=P("section", "fsdp", "tp"),
        check_vma=False,
    )
```

```python
import functools

import jax
import jax.numpy as jnp
from jax import lax
from jax.experimental import pallas as pl
from jax.experimental.pallas import tpu as pltpu
from jax.sharding import PartitionSpec as P

HD = 128
IMG = 256
NX, NZ, LINE = 4, 8, 4
LOG2E = 1.4426950408889634
TROWS = 80
BF16 = jnp.bfloat16
F32 = jnp.float32
AXES = ("fsdp", "tp")


def place(x, z, core):
    return ((x * 2 + z // LINE) * 2 + core) * LINE + z % LINE


def shift(value, dx=0, dz=0, dcore=0):
    pairs = []
    for x in range(NX):
        for z in range(NZ):
            for core in range(2):
                to = place((x + dx) % NX, (z + dz) % NZ, (core + dcore) % 2)
                pairs.append((place(x, z, core), to))
    return lax.ppermute(value, AXES, pairs)


def rotate(value, axis, step):
    return lax.ppermute(value, axis, [(i, (i + step) % 4) for i in range(4)])


def after(value, *others):
    return lax.optimization_barrier((value, *others))[0] if others else value


def transposed(value, dz=0):
    pairs = []
    for x in range(NX):
        for z in range(NZ):
            for core in range(2):
                to = place(z % LINE, (z // LINE * LINE + x + dz) % NZ, core)
                pairs.append((place(x, z, core), to))
    return lax.ppermute(value, AXES, pairs)


def x_all(block, *gate):
    block = after(block, *gate)
    return [block] + [shift(block, dx=d) for d in (1, -1, 2)]


def x_gather(block):
    return lax.all_gather(
        block, "fsdp", axis_index_groups=[[4 * x + rest for x in range(NX)] for rest in range(4)])


def block_parts(refs, depth):
    out = []
    for ref in refs:
        for view in [ref] if len(ref.shape) == 2 else [ref.at[i] for i in range(ref.shape[0])]:
            out += [view.at[pl.ds(i * depth, depth)] for i in range(view.shape[0] // depth)]
    return out


def text_kernel(table, text_own, text_other, from_low, from_high, *rest):
    outs, (w, text, w_sem, t_sem) = rest[:4], rest[4:]
    copies = []
    for j, part in enumerate(block_parts((from_low, from_high), 256)):
        at = pl.multiple_of(table[j] * 256, 256)
        copies.append(pltpu.make_async_copy(part, w.at[pl.ds(at, 256)], w_sem.at[j]))
    for g, source in enumerate((text_own, text_other)):
        for r in range(4):
            copies.append(pltpu.make_async_copy(
                source.at[-r % 4], text.at[r, pl.ds(g * TROWS, TROWS)], t_sem.at[4 * g + r]))
    for copy in copies:
        copy.start()
    for copy in copies:
        copy.wait()
    for r in range(4):
        outs[r][...] = jnp.dot(
            text[r], w[...], preferred_element_type=F32).astype(outs[r].dtype)


def project_text(table, texts, weights):
    smem = pl.BlockSpec(memory_space=pltpu.SMEM)
    hbm = pl.BlockSpec(memory_space=pltpu.HBM)
    return pl.pallas_call(
        text_kernel,
        out_shape=[jax.ShapeDtypeStruct((2 * TROWS, 4 * HD), F32 if r == 0 else BF16)
                   for r in range(4)],
        in_specs=[smem] + [hbm] * 4,
        out_specs=[pl.BlockSpec(memory_space=pltpu.VMEM)] * 4,
        scratch_shapes=[
            pltpu.VMEM((1024, 4 * HD), BF16),
            pltpu.VMEM((4, 2 * TROWS, 1024), BF16),
            pltpu.SemaphoreType.DMA((4,)),
            pltpu.SemaphoreType.DMA((8,)),
        ],
        compiler_params=pltpu.CompilerParams(vmem_limit_bytes=24 * 2**20),
        cost_estimate=pl.CostEstimate(
            flops=2 * 640 * 1024 * 512, bytes_accessed=4 * 2**20, transcendentals=0),
    )(table, *texts, *weights)


def head_kernel(side, table, lengths, image_own, image_other, *rest):
    parts, weights = rest[:4], rest[4:-10]
    out, w, rows, text, sent, tkv, qkv, w_sem, t_sem, i_sem = rest[-10:]
    depth = 256
    copies = []
    for j, part in enumerate(block_parts(weights, depth)):
        at = pl.multiple_of(table[j] * depth, depth)
        copies.append(pltpu.make_async_copy(part, w.at[pl.ds(at, depth)], w_sem.at[j]))
    for r in range(4):
        copies.append(pltpu.make_async_copy(
            parts[r].at[:, pl.ds(side * 2 * HD, 2 * HD)], text if r == 0 else sent.at[r - 1],
            t_sem.at[r]))
    for copy in copies:
        copy.start()
    def fetch(k):
        source = image_own if k < 3 else image_other
        return pltpu.make_async_copy(
            source.at[pl.ds((k - k // 3 * 3) * IMG, IMG)],
            rows.at[k // 3, pl.ds((k - k // 3 * 3) * IMG, IMG)], i_sem.at[k])

    for k in range(2):
        fetch(k).start()
    for copy in copies:
        copy.wait()
    text_kv = (text[...] + sent[0].astype(F32) + sent[1].astype(F32)
               + sent[2].astype(F32)).astype(BF16)
    tkv[...] = jnp.zeros_like(tkv)
    for g in range(2):
        tkv[g, 0:TROWS, :] = text_kv[g * TROWS:(g + 1) * TROWS]

    def compute(k):
        g = k // 3
        here = pl.ds(pl.multiple_of((k - 3 * g) * IMG, IMG), IMG)
        qkv[k % 2] = jnp.dot(rows[g, here], w[...], preferred_element_type=F32).astype(BF16)

    def mix(k):
        g = k // 3
        j = k - 3 * g
        q, key, value = qkv[k % 2, :, :HD], qkv[k % 2, :, HD:2 * HD], qkv[k % 2, :, 2 * HD:]
        first = lengths[g, 0]
        second = first + lengths[g, 1]
        low = jnp.where(j == 0, 0, jnp.where(j == 1, first, second))
        high = jnp.where(j == 0, first, jnp.where(j == 1, second, 72))
        tk, tv = tkv[g, :, :HD], tkv[g, :, HD:]
        dims = (((1,), (1,)), ((), ()))
        scale = HD ** (-0.5) * LOG2E
        s_image = lax.dot_general(q, key, dims, preferred_element_type=F32) * scale
        s_text = lax.dot_general(q, tk, dims, preferred_element_type=F32) * scale
        position = lax.broadcasted_iota(jnp.int32, s_text.shape, 1)
        seen = (position >= low) & (position < high)
        s_text = jnp.where(seen, s_text, -jnp.inf)
        top = jnp.maximum(jnp.max(s_image, axis=1, keepdims=True),
                          jnp.max(s_text, axis=1, keepdims=True))
        e_image = jnp.exp2(s_image - top)
        e_text = jnp.exp2(s_text - top)
        total = (jnp.sum(e_image, axis=1, keepdims=True)
                 + jnp.sum(e_text, axis=1, keepdims=True))
        inverse = 1.0 / total
        mixed = jnp.dot((e_image * inverse).astype(BF16), value, preferred_element_type=F32)
        mixed += jnp.dot((e_text * inverse).astype(BF16), tv, preferred_element_type=F32)
        out[k] = mixed.astype(BF16)

    for k in range(6):
        if k + 2 < 6:
            fetch(k + 2).start()
        fetch(k).wait()
        compute(k)
        if k > 0:
            mix(k - 1)
    mix(5)


def attend(side, table, lengths, images, parts, weights):
    smem = pl.BlockSpec(memory_space=pltpu.SMEM)
    hbm = pl.BlockSpec(memory_space=pltpu.HBM)
    return pl.pallas_call(
        functools.partial(head_kernel, side),
        out_shape=jax.ShapeDtypeStruct((6, IMG, HD), BF16),
        in_specs=[smem] * 2 + [hbm] * (6 + len(weights)),
        out_specs=pl.BlockSpec(memory_space=pltpu.VMEM),
        scratch_shapes=[
            pltpu.VMEM((4096, 3 * HD), BF16),
            pltpu.VMEM((2, 3 * IMG, 4096), BF16),
            pltpu.VMEM((2 * TROWS, 2 * HD), F32),
            pltpu.VMEM((3, 2 * TROWS, 2 * HD), BF16),
            pltpu.VMEM((2, 128, 2 * HD), BF16),
            pltpu.VMEM((2, IMG, 3 * HD), BF16),
            pltpu.SemaphoreType.DMA((16,)),
            pltpu.SemaphoreType.DMA((4,)),
            pltpu.SemaphoreType.DMA((6,)),
        ],
        compiler_params=pltpu.CompilerParams(vmem_limit_bytes=48 * 2**20),
        cost_estimate=pl.CostEstimate(
            flops=2 * 1536 * 4096 * 512, bytes_accessed=16 * 2**20, transcendentals=6 * 256 * 384),
    )(table, lengths, *images, *parts, *weights)


def out_kernel(spots, heads, *rest):
    mixed_parts, rest = rest[:2], rest[2:]
    stacks, (out, w, m, total, w_sem, m_sem) = rest[:2], rest[2:]
    w_copies, m_copies = [], []
    for n, part in enumerate(block_parts(stacks, 512)):
        at = pl.multiple_of(spots[n, 1] * 256, 256)
        w_copies.append(pltpu.make_async_copy(
            part, w.at[spots[n, 0], :, pl.ds(at, 256)], w_sem.at[n]))
    for r in range(LINE):
        for h in range(2):
            for s in range(2):
                at = pl.multiple_of((heads[s] + h) * HD, HD)
                m_copies.append(pltpu.make_async_copy(
                    mixed_parts[h].at[r, :, pl.ds(s * HD, HD)],
                    m.at[r, :, pl.ds(at, HD)], m_sem.at[4 * r + 2 * h + s]))
    for copy in w_copies + m_copies:
        copy.start()
    for copy in w_copies:
        copy.wait()
    for r in range(LINE):
        for copy in m_copies[4 * r:4 * r + 4]:
            copy.wait()
        for k in range(3):
            at = slice(256 * k, 256 * k + 256)
            term = jnp.dot(m[r, at, :], w[(r + 2) % LINE], preferred_element_type=F32)
            term = term.astype(BF16).astype(F32)
            if r == 0:
                total[at, :] = term
            elif r < LINE - 1:
                total[at, :] += term
            else:
                out[at, :] = (total[at, :] + term).astype(BF16)


def project(spots, heads, mixed_parts, stacks):
    smem = pl.BlockSpec(memory_space=pltpu.SMEM)
    hbm = pl.BlockSpec(memory_space=pltpu.HBM)
    return pl.pallas_call(
        out_kernel,
        out_shape=jax.ShapeDtypeStruct((768, 1024), BF16),
        in_specs=[smem] * 2 + [hbm] * 4,
        out_specs=pl.BlockSpec(memory_space=pltpu.VMEM),
        scratch_shapes=[
            pltpu.VMEM((LINE, 512, 1024), BF16),
            pltpu.VMEM((LINE, 768, 512), BF16),
            pltpu.VMEM((768, 1024), F32),
            pltpu.SemaphoreType.DMA((16,)),
            pltpu.SemaphoreType.DMA((16,)),
        ],
        compiler_params=pltpu.CompilerParams(vmem_limit_bytes=48 * 2**20),
        cost_estimate=pl.CostEstimate(
            flops=2 * 768 * 2048 * 1024, bytes_accessed=9 * 2**20, transcendentals=0),
    )(spots, heads, *mixed_parts, *stacks)


def body(image, text_states, caption_lengths, layer_map, w_qkv, w_text_kv, w_out):
    y = lax.axis_index("section")
    f = lax.axis_index("fsdp")
    t = lax.axis_index("tp")
    x, z, core = f // 4, (f // 2) % 2 * LINE + t, f % 2

    image_weight = w_qkv[0].reshape(256, 3, 4, HD)
    text_weight = w_text_kv[0].reshape(256, 2, 4, HD)

    def head_columns(side):
        heads = [2 * side, 2 * side + 1]
        return jnp.concatenate(
            [image_weight[:, i, n] for n in heads for i in range(3)]
            + [text_weight[:, i, n] for n in heads for i in range(2)], axis=1)

    side0, side1 = head_columns(0), head_columns(1)
    sent = jnp.concatenate(
        [lax.select(core == 0, side1, side0),
         jnp.pad(caption_lengths.astype(BF16), ((0, 15), (0, 10 * HD - 3)))])
    got = shift(sent, dcore=1)
    lengths = jnp.concatenate([caption_lengths, got[256:257, :3].astype(jnp.int32)])
    both = jnp.concatenate([lax.select(core == 0, side0, side1), got[:256]])
    cuts = [both[:, :3 * HD], both[:, 3 * HD:6 * HD], both[:, 6 * HD:]]

    chosen = lax.dynamic_index_in_dim(layer_map, y, 0, keepdims=False)
    text_here = jnp.pad(text_states[0], ((0, TROWS - 72), (0, 0)))
    options = [text_here] + [rotate(text_here, "section", -r) for r in (1, 2, 3)]
    picked = lax.select_n((chosen - y) % 4, *options)

    def z_pair(block, *gate):
        block = after(block, *gate)
        return [shift(block, dz=2), shift(block, dz=-2)]

    wide = jnp.stack([picked] + [rotate(picked, "tp", r) for r in (1, 2, 3)])
    pair0 = z_pair(cuts[0], got, picked)

    weights0 = x_gather(jnp.concatenate(pair0))
    slices = [lax.dynamic_index_in_dim(wide, (t - x - d) % 4, 0, keepdims=False) for d in range(4)]
    text_own = jnp.stack(slices[:1] + [shift(slices[d], dx=d) for d in (1, 2, 3)])
    pair_text = z_pair(cuts[2], wide, *pair0)
    images = [image[0], shift(after(image[0], wide, got), dcore=1)]

    texts = [text_own, shift(after(text_own, *pair_text), dcore=1)]

    def rows_at(source, dz):
        chip = source % 4 * 4 + (z + dz) % NZ // LINE * 2
        return [chip + core, chip + 1 - core]

    def table_of(sources):
        rows = [row for source in sources for dz in (-2, 2) for row in rows_at(source, dz)]
        return jnp.stack(rows).astype(jnp.int32)

    text_parts = list(project_text(table_of([x]) % 4, texts, pair_text))
    text_parts = text_parts[:1] + [shift(text_parts[r], dx=r) for r in (1, 2, 3)]
    pair1 = z_pair(cuts[1], texts[1])

    weights1 = x_gather(jnp.concatenate(pair1))
    w_out_here = after(w_out[0], *text_parts[1:])
    pieces = jnp.concatenate([transposed(w_out_here), transposed(w_out_here, dz=4)])
    mixed0 = attend(
        0, table_of(range(NX)), lengths, images,
        [text_parts[0], *after(tuple(text_parts[1:]), *pair1)], [weights0])

    def swap_rows(mixed):
        swapped = shift(mixed[3:].reshape(768, HD), dcore=1)
        return jnp.concatenate([mixed[:3].reshape(768, HD), swapped], axis=1)

    mine0 = swap_rows(mixed0)
    mixed1 = attend(
        1, after(table_of(range(NX)), mine0), lengths, images, text_parts, [weights1])

    mine1 = swap_rows(mixed1)
    mixed_parts = [lax.all_gather(mine0, "tp"), lax.all_gather(mine1, "tp")]
    stack = jnp.concatenate(x_all(pieces, mine1))
    stacks = [stack, shift(stack, dcore=1)]
    spots = []
    for other in range(2):
        for dx in (0, -1, 1, 2):
            for dz in (0, 4):
                spots.append(jnp.stack(
                    [(x + dx) % 4, (z + dz) % NZ // LINE * 2 + (core + other) % 2]))
    spots = jnp.stack(spots).astype(jnp.int32)
    heads = jnp.stack([2 * core, 2 - 2 * core]).astype(jnp.int32)
    return project(spots, heads, mixed_parts, stacks)[None]


def solution(mesh):
    return jax.shard_map(
        body,
        mesh=mesh,
        in_specs=(
            P("section", "fsdp", None),
            P("section", "fsdp", "tp"),
            P("fsdp", None),
            P(),
            P("section", "fsdp", None, "tp"),
            P("section", "fsdp", None, "tp"),
            P("section", "tp", "fsdp"),
        ),
        out_specs=P("section", "fsdp", "tp"),
        check_vma=False,
    )
```
